512 devices in a mesh: seq: 64 (over y_hi, z, x), mp: 8 (over y_lo, core).
Axes of the slice: x: 4, y: 8 (y_hi: 2, y_lo: 4; y = y_hi * 4 + y_lo), z: 8, core: 2. Of those that a mesh axis runs over, the one named last changes fastest.
Arguments:
- queries: bfloat16 [32768, 4096], P(('seq', 'mp')), may hold values from -6 to 6
- memory_keys: bfloat16 [512, 4096], P('seq', 'mp'), may hold values from -6 to 6
- memory_values: bfloat16 [512, 4096], P('seq', 'mp'), may hold values from -48 to 48
- output_grad: bfloat16 [32768, 4096], P(('seq', 'mp')), may hold values from -24 to 24
Outputs:
- attended: bfloat16 [32768, 4096], P(('seq', 'mp'))
- query_grad: bfloat16 [32768, 4096], P(('seq', 'mp'))
- key_grad: bfloat16 [512, 4096], P('seq', 'mp')
- value_grad: bfloat16 [512, 4096], P('seq', 'mp')
The draws below stay inside these ranges and needn't reach their ends.
All inputs are finite; a program needn't handle non-finite values.
Results may differ from the reference program's by a relative error of at most 0.012.
The reference program's roundings to bfloat16 on the way (of `attention_weights` and `score_grad`) count: a program that leaves them out, or rounds other values in their place, can miss the bound.
Values may be sent and summed in bfloat16 or wider, within the bound.
A program may use at most 64 MiB of HBM per device.

```python
import math
import jax
import jax.numpy as jnp
from jax import lax

DH = 128
FEATURES = 4096
LENGTH = 32768
MEMORY = 512


def draw_memory_keys(key, part):
    key = jax.random.fold_in(key, 7)
    base = jnp.clip(jax.random.normal(key, (MEMORY, FEATURES), jnp.float32), -4.0, 4.0)
    return base.astype(jnp.bfloat16)


def draw_queries(key, part):
    key = jax.random.fold_in(key, 5)
    base = jnp.clip(jax.random.normal(key, (LENGTH, FEATURES), jnp.float32), -4.0, 4.0)
    return base.astype(jnp.bfloat16)


def block_scale(key, extent, shards, least, top_value):
    level, own = 1.0, jax.random.fold_in(key, 6)
    for dim, blocks in shards:
        steps = jnp.exp(jax.random.uniform(jax.random.fold_in(own, dim), (blocks,), jnp.float32, least / len(shards), top_value / len(shards)))
        level = level * jnp.repeat(steps, extent[dim] // blocks).reshape([-1 if axis == dim else 1 for axis in range(len(extent))])
    return level


def noise(own_key, dims, spread, limit, split=(), dtype=jnp.bfloat16):
    level = block_scale(own_key, dims, split, -0.22, 0.18) if split else 1.0
    array = jax.random.normal(own_key, dims, jnp.float32) * spread * level
    return jnp.minimum(jnp.maximum(array, -limit), limit).astype(dtype)


def setup_inputs(seed: int = 0) -> dict:
    arg_keys = jax.random.split(jax.random.key(seed), 5)
    queries = draw_queries(jax.random.fold_in(arg_keys[4], 71), 0)
    memory_keys = draw_memory_keys(jax.random.fold_in(arg_keys[4], 71), 0)
    memory_values = noise(arg_keys[2], (MEMORY, FEATURES), 8.0, 48.0, ((0, 64), (1, 8)))
    output_grad = noise(arg_keys[3], (LENGTH, FEATURES), 4.0, 24.0, ((0, 512),))
    return dict(queries=queries, memory_keys=memory_keys, memory_values=memory_values, output_grad=output_grad)


def split_heads(matrix, head_width):
    row_count = matrix.shape[0]
    return matrix.reshape(row_count, -1, head_width).transpose(1, 0, 2)

def join_heads(stacked):
    head_count, row_count, head_width = stacked.shape
    return stacked.transpose(1, 0, 2).reshape(row_count, head_count * head_width)

def forward_head(query_rows, key_rows, value_rows):
    temper = 1.0 / math.sqrt(query_rows.shape[1])
    scores = jnp.dot(query_rows, key_rows.T, preferred_element_type=jnp.float32) * temper
    peak_score = lax.optimization_barrier(jnp.max(scores, axis=1, keepdims=True))
    log_total = peak_score + jnp.log(lax.optimization_barrier(jnp.sum(jnp.exp(scores - peak_score), axis=1, keepdims=True)))
    attention_weights = jnp.exp(scores - log_total).astype(jnp.bfloat16)
    attended = jnp.dot(attention_weights, value_rows, preferred_element_type=jnp.float32).astype(jnp.bfloat16)
    return (attended, log_total)

def backward_head(query_rows, key_rows, value_rows, grad_rows, attended, log_total):
    temper = 1.0 / math.sqrt(query_rows.shape[1])
    scores = jnp.dot(query_rows, key_rows.T, preferred_element_type=jnp.float32) * temper
    exact_weights = jnp.exp(scores - log_total)
    attention_weights = exact_weights.astype(jnp.bfloat16)
    row_delta = lax.optimization_barrier(jnp.sum(grad_rows.astype(jnp.float32) * attended.astype(jnp.float32), axis=1, keepdims=True))
    prob_grad = jnp.dot(grad_rows, value_rows.T, preferred_element_type=jnp.float32)
    score_grad = (exact_weights * (prob_grad - row_delta) * temper).astype(jnp.bfloat16)
    query_grad = jnp.dot(score_grad, key_rows, preferred_element_type=jnp.float32).astype(jnp.bfloat16)
    key_grad = jnp.dot(score_grad.T, query_rows, preferred_element_type=jnp.float32)
    value_grad = jnp.dot(attention_weights.T, grad_rows, preferred_element_type=jnp.float32)
    return (query_grad, key_grad, value_grad)

def one_head(operands):
    query_rows, key_rows, value_rows, grad_rows = operands
    attended, log_total = forward_head(query_rows, key_rows, value_rows)
    query_grad, key_grad, value_grad = backward_head(query_rows, key_rows, value_rows, grad_rows, attended, log_total)
    return (attended, query_grad, key_grad.astype(jnp.bfloat16), value_grad.astype(jnp.bfloat16))

def reference(queries, memory_keys, memory_values, output_grad):
    stacked = (split_heads(queries, DH), split_heads(memory_keys, DH), split_heads(memory_values, DH), split_heads(output_grad, DH))
    attended, query_grad, key_grad, value_grad = lax.map(one_head, stacked)
    return (join_heads(attended), join_heads(query_grad), join_heads(key_grad), join_heads(value_grad))
```

```python
import math

import jax
import jax.numpy as jnp
from jax import lax
from jax.experimental import pallas as pl
from jax.experimental.pallas import tpu as pltpu
from jax.sharding import PartitionSpec as P

MESH = pl.DeviceIdType.MESH
DH = 128
TEMPER = 1.0 / math.sqrt(DH)
LOG2E = 1.0 / math.log(2.0)
NT = (((1,), (1,)), ((), ()))
BF16, F32 = jnp.bfloat16, jnp.float32
TILES, PER_TILE, TOKENS = 4, 4, 64
TILE = PER_TILE * TOKENS


def place():
    seq, mp = lax.axis_index("seq"), lax.axis_index("mp")
    return seq % 4, (seq // 32) * 4 + mp // 2, (seq // 4) % 8, mp % 2


def device(x, y, z, core):
    return (y // 4) * 32 + z * 4 + x, (y % 4) * 2 + core


def kernel(
    q, k, v, g, att, dq, kg, vg,
    qb, gb, kvsrc, kv, attb, dqb, kc, vc, kt, vt, dk, dv, part, own, landf, landh, red, landb,
    in_send, in_recv, loc, kv1_send, kv1_recv, kv2_send, kv2_recv, out_send, out_recv,
    a_send, a_recv, b_send, b_recv,
):
    x, y, z, core = place()
    yh, a = y // 4, y % 4
    zp, zb = z // 2, z % 2
    pair = 4 * x + 2 * core + zb
    on_diagonal = x == a

    def group(i, sign):
        dx, dz, dc = i // 4, (i // 2) % 2, i % 2
        xx, bb, cc = (x + sign * dx + 4) % 4, (zb + dz) % 2, (core + dc) % 2
        return device(xx, y, 2 * zp + bb, cc), 4 * xx + 2 * cc + bb

    def across(i):
        return i // 8, i % 8, device(a, (i // 8) * 4 + x, i % 8, core)

    def along(d):
        return device(x, (y + d + 8) % 8, z, core)

    def remote(src, dst, send, recv, to):
        return pltpu.make_async_remote_copy(
            src_ref=src, dst_ref=dst, send_sem=send, recv_sem=recv, device_id=to, device_id_type=MESH
        )

    def bytes_of(ref, sem):
        pltpu.make_async_copy(ref, ref, sem).wait()

    def is_me(i):
        return on_diagonal & (i // 8 == yh) & (i % 8 == z)

    def columns(head_pair, head):
        return pl.ds(pl.multiple_of(head_pair * 256 + head * 128, 128), 128)

    barrier = pltpu.get_barrier_semaphore()

    def greet(to):
        pl.semaphore_signal(barrier, inc=1, device_id=to, device_id_type=MESH)

    @pl.loop(0, 16)
    def _(i):
        @pl.when(jnp.logical_not(is_me(i)))
        def _():
            greet(across(i)[2])

    @pl.loop(1, 16)
    def _(i):
        greet(group(i, 1)[0])

    for d in (1, -1, 2, -2):
        greet(along(d))

    mine = []
    for h in range(2):
        for n, (src, dst) in enumerate(((q, qb), (g, gb))):
            mine.append(pltpu.make_async_copy(src.at[:, columns(pair, h)], dst.at[h, 0], loc.at[n, h]))
            mine[-1].start()
    for h in range(4):
        kvsrc[h] = jnp.concatenate(
            [k[:, h * DH : (h + 1) * DH].astype(F32), v[:, h * DH : (h + 1) * DH].astype(F32)], axis=0
        ).astype(BF16)

    pl.semaphore_wait(barrier, 35 - on_diagonal.astype(jnp.int32))

    @pl.loop(0, 16)
    def _(i):
        h, zz, to = across(i)
        half = kvsrc.at[pl.ds((zz % 2) * 2, 2)]
        dst = kv.at[:, x, yh * 8 + z]

        @pl.when(jnp.logical_not(is_me(i)))
        def _():
            remote(half, dst, kv1_send, kv1_recv, to).start()

        @pl.when(is_me(i))
        def _():
            copy = pltpu.make_async_copy(half, dst, loc.at[2, 0])
            copy.start()
            copy.wait()

    for h in range(2):
        for t in range(TILES):
            for i in range(max(1, t * PER_TILE), (t + 1) * PER_TILE):
                to, theirs = group(i, 1)
                for n, (src, dst) in enumerate(((q, qb), (g, gb))):
                    remote(src.at[:, columns(theirs, h)], dst.at[h, i], in_send, in_recv.at[h, t, n], to).start()

    @pl.when(on_diagonal)
    def _():
        bytes_of(kv.at[:, 0, pl.ds(0, 15)], kv1_recv)

    @pl.when(jnp.logical_not(on_diagonal))
    def _():
        bytes_of(kv.at[:, 0], kv1_recv)

    lower, upper = pl.ds(0, 8), pl.ds(8, 8)
    for h in range(2):
        for piece, d in ((pl.ds(0, 16), 1), (pl.ds(0, 16), -1), (lower, 2), (upper, -2)):
            ref = kv.at[h, a, piece]
            remote(ref, ref, kv2_send, kv2_recv.at[h], along(d)).start()

    for h in range(2):
        bytes_of(kv.at[h, pl.ds(0, 3)], kv2_recv.at[h])
        both = kv[h].reshape(64, 16, DH).astype(F32)
        keys = both[:, :8].reshape(512, DH)
        values = both[:, 8:].reshape(512, DH)
        kc[...] = keys.astype(BF16)
        vc[...] = values.astype(BF16)
        kt[...] = keys.T.astype(BF16)
        vt[...] = values.T.astype(BF16)
        for copy in mine[2 * h : 2 * h + 2]:
            copy.wait()
        for t in range(TILES):
            for n, dst in enumerate((qb, gb)):
                bytes_of(dst.at[h, pl.ds(0, 3 if t == 0 else 4)], in_recv.at[h, t, n])
            rows = pl.ds(t * PER_TILE, PER_TILE)
            qt = qb[h, rows].reshape(TILE, DH)
            gt = gb[h, rows].reshape(TILE, DH)
            s = lax.dot_general(kc[...], qt, NT, preferred_element_type=F32)
            dp = lax.dot_general(vc[...], gt, NT, preferred_element_type=F32)
            top = jnp.max(s, axis=0, keepdims=True)
            e = jnp.exp2((s - top) * (TEMPER * LOG2E))
            inverse = 1.0 / jnp.sum(e, axis=0, keepdims=True)
            delta = jnp.sum(e * dp, axis=0, keepdims=True) * inverse
            p = (e * inverse).astype(BF16)
            ds = (e * (dp - delta) * (inverse * TEMPER)).astype(BF16)
            attb[h, rows] = (
                jnp.dot(vt[...], p, preferred_element_type=F32).T.astype(BF16).reshape(PER_TILE, TOKENS, DH)
            )
            dqb[h, rows] = (
                jnp.dot(kt[...], ds, preferred_element_type=F32).T.astype(BF16).reshape(PER_TILE, TOKENS, DH)
            )
            for i in range(t * PER_TILE, (t + 1) * PER_TILE):
                for n, (src, dst) in enumerate(((attb, att), (dqb, dq))):
                    target = dst.at[:, columns(pair, h)]
                    if i:
                        remote(src.at[h, i], target, out_send, out_recv.at[n], group(i, -1)[0]).start()
                    else:
                        pltpu.make_async_copy(src.at[h, i], target, loc.at[n, 2 + h]).start()
            dk_t = jnp.dot(ds, qt, preferred_element_type=F32)
            dv_t = jnp.dot(p, gt, preferred_element_type=F32)
            if t == 0:
                dk[...] = dk_t
                dv[...] = dv_t
            else:
                dk[...] += dk_t
                dv[...] += dv_t
        whole = jnp.concatenate([dk[...].reshape(64, 8, DH), dv[...].reshape(64, 8, DH)], axis=1)
        own[h] = whole.reshape(4, 16, 16, DH)
        part[h] = whole.astype(BF16).reshape(4, 16, 16, DH)
        for n, d in enumerate((1, -1)):
            remote(part.at[h, (a + d + 4) % 4], landf.at[h, n], a_send, a_recv.at[h, 0], along(d)).start()
        for n, d in enumerate((-2, 2)):
            remote(
                part.at[h, (a + 2) % 4, pl.ds(n * 8, 8)], landh.at[h, n], a_send, a_recv.at[h, 1], along(d)
            ).start()

    for h in range(2):
        bytes_of(landf.at[h], a_recv.at[h, 0])
        bytes_of(landh.at[h], a_recv.at[h, 1])
        total = own[h, a] + landf[h, 0].astype(F32) + landf[h, 1].astype(F32)
        total += landh[h].astype(F32).reshape(16, 16, DH)
        red[:, h] = total.astype(BF16)

        @pl.loop(0, 16)
        def _(i):
            hh, zz, to = across(i)
            dst = landb.at[yh * 4 + zp, zb * 2 + h]

            @pl.when(jnp.logical_not(is_me(i)))
            def _():
                remote(red.at[i, h], dst, b_send, b_recv, to).start()

            @pl.when(is_me(i))
            def _():
                copy = pltpu.make_async_copy(red.at[i, h], dst, loc.at[2, 1])
                copy.start()
                copy.wait()

    for n, (src, dst) in enumerate(((attb, att), (dqb, dq))):
        for h in range(2):
            pltpu.make_async_copy(src.at[h, 0], dst.at[:, columns(pair, h)], loc.at[n, 2 + h]).wait()

    for sem in (b_recv, b_send):

        @pl.when(on_diagonal)
        def _():
            bytes_of(red.at[pl.ds(0, 15)], sem)

        @pl.when(jnp.logical_not(on_diagonal))
        def _():
            bytes_of(red, sem)

    final = landb[0].astype(F32)
    for n in range(1, 8):
        final += landb[n].astype(F32)
    for h in range(4):
        kg[:, h * DH : (h + 1) * DH] = final[h, :8].astype(BF16)
        vg[:, h * DH : (h + 1) * DH] = final[h, 8:].astype(BF16)

    for n in range(2):
        bytes_of(attb.at[:, pl.ds(0, 15)], out_recv.at[n])
        bytes_of(attb.at[:, pl.ds(0, 15)], out_send)
        bytes_of(qb.at[:, pl.ds(0, 15)], in_send)
        bytes_of(kv.at[0, pl.ds(0, 3)], kv2_send)
        bytes_of(kv.at[0, pl.ds(0, 3)], a_send)

    @pl.when(on_diagonal)
    def _():
        bytes_of(kv.at[:, 0, pl.ds(0, 15)], kv1_send)

    @pl.when(jnp.logical_not(on_diagonal))
    def _():
        bytes_of(kv.at[:, 0], kv1_send)


def shards(queries, memory_keys, memory_values, output_grad):
    vmem, hbm = pl.BlockSpec(memory_space=pltpu.VMEM), pl.BlockSpec(memory_space=pl.ANY)
    tokens, memory = jax.ShapeDtypeStruct((64, 4096), BF16), jax.ShapeDtypeStruct((8, 512), BF16)
    dma = pltpu.SemaphoreType.DMA
    return pl.pallas_call(
        kernel,
        name="attention",
        out_shape=(tokens, tokens, memory, memory),
        in_specs=[hbm, vmem, vmem, hbm],
        out_specs=(hbm, hbm, vmem, vmem),
        scratch_shapes=[
            pltpu.VMEM((2, 16, TOKENS, DH), BF16),
            pltpu.VMEM((2, 16, TOKENS, DH), BF16),
            pltpu.VMEM((4, 16, DH), BF16),
            pltpu.VMEM((2, 4, 16, 16, DH), BF16),
            pltpu.VMEM((2, 16, TOKENS, DH), BF16),
            pltpu.VMEM((2, 16, TOKENS, DH), BF16),
            pltpu.VMEM((512, DH), BF16),
            pltpu.VMEM((512, DH), BF16),
            pltpu.VMEM((DH, 512), BF16),
            pltpu.VMEM((DH, 512), BF16),
            pltpu.VMEM((512, DH), F32),
            pltpu.VMEM((512, DH), F32),
            pltpu.VMEM((2, 4, 16, 16, DH), BF16),
            pltpu.VMEM((2, 4, 16, 16, DH), F32),
            pltpu.VMEM((2, 2, 16, 16, DH), BF16),
            pltpu.VMEM((2, 2, 8, 16, DH), BF16),
            pltpu.VMEM((16, 2, 16, DH), BF16),
            pltpu.VMEM((8, 4, 16, DH), BF16),
            dma,
            dma((2, TILES, 2)),
            dma((3, 4)),
            dma,
            dma,
            dma,
            dma((2,)),
            dma,
            dma((2,)),
            dma,
            dma((2, 2)),
            dma,
            dma,
        ],
        compiler_params=pltpu.CompilerParams(
            collective_id=0, has_side_effects=True, vmem_limit_bytes=40 * 2**20
        ),
    )(queries, memory_keys, memory_values, output_grad)


def solution(mesh):
    return jax.shard_map(
        shards,
        mesh=mesh,
        in_specs=(P(("seq", "mp"), None), P("seq", "mp"), P("seq", "mp"), P(("seq", "mp"), None)),
        out_specs=(P(("seq", "mp"), None), P(("seq", "mp"), None), P("seq", "mp"), P("seq", "mp")),
        check_vma=False,
    )
```

```python
import math

import jax
import jax.numpy as jnp
from jax import lax
from jax.experimental import pallas as pl
from jax.experimental.pallas import tpu as pltpu
from jax.sharding import PartitionSpec as P

MESH = pl.DeviceIdType.MESH
DH = 128
TEMPER = 1.0 / math.sqrt(DH)
LOG2E = 1.0 / math.log(2.0)
NT = (((1,), (1,)), ((), ()))
BF16, F32 = jnp.bfloat16, jnp.float32
TILES, PER_TILE, TOKENS = 4, 4, 64
TILE = PER_TILE * TOKENS


def place():
    seq, mp = lax.axis_index("seq"), lax.axis_index("mp")
    return seq % 4, (seq // 32) * 4 + mp // 2, (seq // 4) % 8, mp % 2


def device(x, y, z, core):
    return (y // 4) * 32 + z * 4 + x, (y % 4) * 2 + core


def kernel(
    q, keys_in, values_in, g, att, dq, landb,
    k, v, qb, gb, kvsrc, kv, attb, dqb, kc, vc, kt, vt, dk, dv, part, own, landf, landh, red,
    in_send, in_recv, loc, kv1_send, kv1_recv, kv2_send, kv2_recv, out_send, out_recv,
    a_send, a_recv, b_send, b_recv,
):
    x, y, z, core = place()
    yh, a = y // 4, y % 4
    zp, zb = z // 2, z % 2
    block = (x + 4 - zp) % 4
    pair = 4 * block + 2 * core + zb
    place_in_block = (x + z) % 4
    to_itself = (block == a) & (place_in_block == a)

    def group(i, sign):
        dx, dz, dc = i // 4, (i // 2) % 2, i % 2
        xx, bb, cc = (x + sign * dx + 4) % 4, (zb + dz) % 2, (core + dc) % 2
        return device(xx, y, 2 * zp + bb, cc), 4 * ((xx + 4 - zp) % 4) + 2 * cc + bb

    def workers(i):
        h, zz = i // 8, i % 8
        return zz % 2, device((a + zz // 2) % 4, 4 * h + place_in_block, zz, core)

    def owners(i):
        h, zz = i // 8, i % 8
        return device((a + 8 - zz) % 4, 4 * h + block, zz, core)

    def along(d):
        return device(x, (y + d + 8) % 8, z, core)

    def remote(src, dst, send, recv, to):
        return pltpu.make_async_remote_copy(
            src_ref=src, dst_ref=dst, send_sem=send, recv_sem=recv, device_id=to, device_id_type=MESH
        )

    def bytes_of(ref, sem):
        pltpu.make_async_copy(ref, ref, sem).wait()

    def is_me(i):
        return to_itself & (i // 8 == yh) & (i % 8 == z)

    def columns(head_pair, head):
        return pl.ds(pl.multiple_of(head_pair * 256 + head * 128, 128), 128)

    barrier = pltpu.get_barrier_semaphore()

    def greet(to):
        pl.semaphore_signal(barrier, inc=1, device_id=to, device_id_type=MESH)

    memory = [
        pltpu.make_async_copy(src, dst, loc.at[2, n + 2]) for n, (src, dst) in enumerate(((keys_in, k), (values_in, v)))
    ]
    for copy in memory:
        copy.start()

    @pl.loop(0, 16)
    def _(i):
        @pl.when(jnp.logical_not(is_me(i)))
        def _():
            greet(workers(i)[1])
            greet(owners(i))

    @pl.loop(1, 16)
    def _(i):
        greet(group(i, 1)[0])

    for d in (1, -1, 2, -2):
        greet(along(d))

    mine = []
    for h in range(2):
        for n, (src, dst) in enumerate(((q, qb), (g, gb))):
            mine.append(pltpu.make_async_copy(src.at[:, columns(pair, h)], dst.at[h, 0], loc.at[n, h]))
            mine[-1].start()
    for copy in memory:
        copy.wait()
    for h in range(4):
        kvsrc[h] = jnp.concatenate(
            [k[:, h * DH : (h + 1) * DH].astype(F32), v[:, h * DH : (h + 1) * DH].astype(F32)], axis=0
        ).astype(BF16)

    pl.semaphore_wait(barrier, 51 - 2 * to_itself.astype(jnp.int32))

    @pl.loop(0, 16)
    def _(i):
        j, to = workers(i)
        half = kvsrc.at[pl.ds(j * 2, 2)]
        dst = kv.at[:, place_in_block, yh * 8 + z]

        @pl.when(jnp.logical_not(is_me(i)))
        def _():
            remote(half, dst, kv1_send, kv1_recv, to).start()

        @pl.when(is_me(i))
        def _():
            copy = pltpu.make_async_copy(half, dst, loc.at[2, 0])
            copy.start()
            copy.wait()

    for h in range(2):
        for t in range(TILES):
            for i in range(max(1, t * PER_TILE), (t + 1) * PER_TILE):
                to, theirs = group(i, 1)
                for n, (src, dst) in enumerate(((q, qb), (g, gb))):
                    remote(src.at[:, columns(theirs, h)], dst.at[h, i], in_send, in_recv.at[h, t, n], to).start()

    @pl.when(to_itself)
    def _():
        bytes_of(kv.at[:, 0, pl.ds(0, 15)], kv1_recv)

    @pl.when(jnp.logical_not(to_itself))
    def _():
        bytes_of(kv.at[:, 0], kv1_recv)

    lower, upper = pl.ds(0, 8), pl.ds(8, 8)
    for h in range(2):
        for piece, d in ((pl.ds(0, 16), 1), (pl.ds(0, 16), -1), (lower, 2), (upper, -2)):
            ref = kv.at[h, a, piece]
            remote(ref, ref, kv2_send, kv2_recv.at[h], along(d)).start()

    for h in range(2):
        bytes_of(kv.at[h, pl.ds(0, 3)], kv2_recv.at[h])
        both = kv[h].reshape(64, 16, DH).astype(F32)
        keys = both[:, :8].reshape(512, DH)
        values = both[:, 8:].reshape(512, DH)
        kc[...] = keys.astype(BF16)
        vc[...] = values.astype(BF16)
        kt[...] = keys.T.astype(BF16)
        vt[...] = values.T.astype(BF16)
        for copy in mine[2 * h : 2 * h + 2]:
            copy.wait()
        for t in range(TILES):
            for n, dst in enumerate((qb, gb)):
                bytes_of(dst.at[h, pl.ds(0, 3 if t == 0 else 4)], in_recv.at[h, t, n])
            rows = pl.ds(t * PER_TILE, PER_TILE)
            qt = qb[h, rows].reshape(TILE, DH)
            gt = gb[h, rows].reshape(TILE, DH)
            s = lax.dot_general(kc[...], qt, NT, preferred_element_type=F32)
            dp = lax.dot_general(vc[...], gt, NT, preferred_element_type=F32)
            top = jnp.max(s, axis=0, keepdims=True)
            e = jnp.exp2((s - top) * (TEMPER * LOG2E))
            inverse = 1.0 / jnp.sum(e, axis=0, keepdims=True)
            delta = jnp.sum(e * dp, axis=0, keepdims=True) * inverse
            p = (e * inverse).astype(BF16)
            ds = (e * (dp - delta) * (inverse * TEMPER)).astype(BF16)
            attb[h, rows] = (
                jnp.dot(vt[...], p, preferred_element_type=F32).T.astype(BF16).reshape(PER_TILE, TOKENS, DH)
            )
            dqb[h, rows] = (
                jnp.dot(kt[...], ds, preferred_element_type=F32).T.astype(BF16).reshape(PER_TILE, TOKENS, DH)
            )
            for i in range(t * PER_TILE, (t + 1) * PER_TILE):
                for n, (src, dst) in enumerate(((attb, att), (dqb, dq))):
                    target = dst.at[:, columns(pair, h)]
                    if i:
                        remote(src.at[h, i], target, out_send, out_recv.at[n], group(i, -1)[0]).start()
                    else:
                        pltpu.make_async_copy(src.at[h, i], target, loc.at[n, 2 + h]).start()
            dk_t = jnp.dot(ds, qt, preferred_element_type=F32)
            dv_t = jnp.dot(p, gt, preferred_element_type=F32)
            if t == 0:
                dk[...] = dk_t
                dv[...] = dv_t
            else:
                dk[...] += dk_t
                dv[...] += dv_t
        whole = jnp.concatenate([dk[...].reshape(64, 8, DH), dv[...].reshape(64, 8, DH)], axis=1)
        own[h] = whole.reshape(4, 16, 16, DH)
        part[h] = whole.astype(BF16).reshape(4, 16, 16, DH)
        for n, d in enumerate((1, -1)):
            remote(part.at[h, (a + d + 4) % 4], landf.at[h, n], a_send, a_recv.at[h, 0], along(d)).start()
        for n, d in enumerate((-2, 2)):
            remote(
                part.at[h, (a + 2) % 4, pl.ds(n * 8, 8)], landh.at[h, n], a_send, a_recv.at[h, 1], along(d)
            ).start()

    for h in range(2):
        bytes_of(landf.at[h], a_recv.at[h, 0])
        bytes_of(landh.at[h], a_recv.at[h, 1])
        total = own[h, a] + landf[h, 0].astype(F32) + landf[h, 1].astype(F32)
        total += landh[h].astype(F32).reshape(16, 16, DH)
        red[:, h] = total.astype(BF16)

        @pl.loop(0, 16)
        def _(i):
            dst = landb.at[yh * 4 + zp, zb * 2 + h]

            @pl.when(jnp.logical_not(is_me(i)))
            def _():
                remote(red.at[i, h], dst, b_send, b_recv, owners(i)).start()

            @pl.when(is_me(i))
            def _():
                copy = pltpu.make_async_copy(red.at[i, h], dst, loc.at[2, 1])
                copy.start()
                copy.wait()

    for n, (src, dst) in enumerate(((attb, att), (dqb, dq))):
        for h in range(2):
            pltpu.make_async_copy(src.at[h, 0], dst.at[:, columns(pair, h)], loc.at[n, 2 + h]).wait()

    for sem in (b_recv, b_send):

        @pl.when(to_itself)
        def _():
            bytes_of(red.at[pl.ds(0, 15)], sem)

        @pl.when(jnp.logical_not(to_itself))
        def _():
            bytes_of(red, sem)

    for n in range(2):
        bytes_of(attb.at[:, pl.ds(0, 15)], out_recv.at[n])
        bytes_of(attb.at[:, pl.ds(0, 15)], out_send)
        bytes_of(qb.at[:, pl.ds(0, 15)], in_send)
        bytes_of(kv.at[0, pl.ds(0, 3)], kv2_send)
        bytes_of(kv.at[0, pl.ds(0, 3)], a_send)

    @pl.when(to_itself)
    def _():
        bytes_of(kv.at[:, 0, pl.ds(0, 15)], kv1_send)

    @pl.when(jnp.logical_not(to_itself))
    def _():
        bytes_of(kv.at[:, 0], kv1_send)


def finish(att_in, dq_in, landb, att, dq, kg, vg, sems):
    copies = [
        pltpu.make_async_copy(src, dst, sems.at[n]) for n, (src, dst) in enumerate(((att_in, att), (dq_in, dq)))
    ]
    for copy in copies:
        copy.start()
    final = landb[0].astype(F32)
    for n in range(1, 8):
        final += landb[n].astype(F32)
    for h in range(4):
        kg[:, h * DH : (h + 1) * DH] = final[h, :8].astype(BF16)
        vg[:, h * DH : (h + 1) * DH] = final[h, 8:].astype(BF16)
    for copy in copies:
        copy.wait()


def shards(queries, memory_keys, memory_values, output_grad):
    vmem, hbm = pl.BlockSpec(memory_space=pltpu.VMEM), pl.BlockSpec(memory_space=pl.ANY)
    tokens, memory = jax.ShapeDtypeStruct((64, 4096), BF16), jax.ShapeDtypeStruct((8, 512), BF16)
    dma = pltpu.SemaphoreType.DMA
    att, dq, landb = pl.pallas_call(
        kernel,
        name="attention",
        out_shape=(pltpu.VMEM((64, 4096), BF16), pltpu.VMEM((64, 4096), BF16), pltpu.VMEM((8, 4, 16, DH), BF16)),
        in_specs=[hbm] * 4,
        out_specs=(vmem, vmem, vmem),
        scratch_shapes=[
            pltpu.VMEM((8, 512), BF16),
            pltpu.VMEM((8, 512), BF16),
            pltpu.VMEM((2, 16, TOKENS, DH), BF16),
            pltpu.VMEM((2, 16, TOKENS, DH), BF16),
            pltpu.VMEM((4, 16, DH), BF16),
            pltpu.VMEM((2, 4, 16, 16, DH), BF16),
            pltpu.VMEM((2, 16, TOKENS, DH), BF16),
            pltpu.VMEM((2, 16, TOKENS, DH), BF16),
            pltpu.VMEM((512, DH), BF16),
            pltpu.VMEM((512, DH), BF16),
            pltpu.VMEM((DH, 512), BF16),
            pltpu.VMEM((DH, 512), BF16),
            pltpu.VMEM((512, DH), F32),
            pltpu.VMEM((512, DH), F32),
            pltpu.VMEM((2, 4, 16, 16, DH), BF16),
            pltpu.VMEM((2, 4, 16, 16, DH), F32),
            pltpu.VMEM((2, 2, 16, 16, DH), BF16),
            pltpu.VMEM((2, 2, 8, 16, DH), BF16),
            pltpu.VMEM((16, 2, 16, DH), BF16),
            dma,
            dma((2, TILES, 2)),
            dma((3, 4)),
            dma,
            dma,
            dma,
            dma((2,)),
            dma,
            dma((2,)),
            dma,
            dma((2, 2)),
            dma,
            dma,
        ],
        compiler_params=pltpu.CompilerParams(
            collective_id=0, has_side_effects=True, vmem_limit_bytes=60 * 2**20
        ),
    )(queries, memory_keys, memory_values, output_grad)
    return pl.pallas_call(
        finish,
        name="finish",
        out_shape=(tokens, tokens, memory, memory),
        in_specs=[vmem, vmem, vmem],
        out_specs=(hbm, hbm, vmem, vmem),
        scratch_shapes=[dma((2,))],
    )(*(pltpu.with_memory_space_constraint(t, pltpu.VMEM) for t in (att, dq, landb)))


def solution(mesh):
    return jax.shard_map(
        shards,
        mesh=mesh,
        in_specs=(P(("seq", "mp"), None), P("seq", "mp"), P("seq", "mp"), P(("seq", "mp"), None)),
        out_specs=(P(("seq", "mp"), None), P(("seq", "mp"), None), P("seq", "mp"), P("seq", "mp")),
        check_vma=False,
    )
```

```python
import math

import jax
import jax.numpy as jnp
from jax import lax
from jax.experimental import pallas as pl
from jax.experimental.pallas import tpu as pltpu
from jax.sharding import PartitionSpec as P

MESH = pl.DeviceIdType.MESH
DH = 128
TEMPER = 1.0 / math.sqrt(DH)
LOG2E = 1.0 / math.log(2.0)
NT = (((1,), (1,)), ((), ()))
BF16, F32 = jnp.bfloat16, jnp.float32
TILES, PER_TILE, TOKENS = 2, 8, 64
SELF = 12
TILE = PER_TILE * TOKENS


def place():
    seq, mp = lax.axis_index("seq"), lax.axis_index("mp")
    return seq % 4, (seq // 32) * 4 + mp // 2, (seq // 4) % 8, mp % 2


def device(x, y, z, core):
    return (y // 4) * 32 + z * 4 + x, (y % 4) * 2 + core


def kernel(
    q, keys_in, values_in, g, att, dq, landb,
    k, v, qb, gb, kvsrc, kv, attb, dqb, kc, vc, kt, vt, pb, dsb, part, own, landf, landh, red,
    in_send, in_recv, loc, kv1_send, kv1_recv, kv2_send, kv2_recv, out_send, out_recv,
    a_send, a_recv, b_send, b_recv,
):
    x, y, z, core = place()
    yh, a = y // 4, y % 4
    zp, zb = z // 2, z % 2
    block = (x + 4 - zp) % 4
    pair = 4 * block + 2 * core + zb
    place_in_block = (x + z) % 4
    to_itself = (block == a) & (place_in_block == a)

    def group(t, k, sign):
        odd, m = k % 2, k // 2 + (k % 2) * t
        dx = 1 + 2 * odd if t == 0 else 2 - 2 * odd
        dz, dc = m // 2, m % 2
        xx, bb, cc = (x + sign * dx + 4) % 4, (zb + dz) % 2, (core + dc) % 2
        return t * PER_TILE + odd * 4 + m, device(xx, y, 2 * zp + bb, cc), 4 * ((xx + 4 - zp) % 4) + 2 * cc + bb

    def workers(i):
        h, zz = i // 8, i % 8
        return zz % 2, device((a + zz // 2) % 4, 4 * h + place_in_block, zz, core)

    def owners(i):
        h, zz = i // 8, i % 8
        return device((a + 8 - zz) % 4, 4 * h + block, zz, core)

    def along(d):
        return device(x, (y + d + 8) % 8, z, core)

    def remote(src, dst, send, recv, to):
        return pltpu.make_async_remote_copy(
            src_ref=src, dst_ref=dst, send_sem=send, recv_sem=recv, device_id=to, device_id_type=MESH
        )

    def bytes_of(ref, sem):
        pltpu.make_async_copy(ref, ref, sem).wait()

    def memory_blocks(ref, sem):
        @pl.when(to_itself)
        def _():
            bytes_of(ref.at[pl.ds(0, 15)], sem)

        @pl.when(jnp.logical_not(to_itself))
        def _():
            bytes_of(ref, sem)

    def is_me(i):
        return to_itself & (i // 8 == yh) & (i % 8 == z)

    def columns(head_pair, head):
        return pl.ds(pl.multiple_of(head_pair * 256 + head * 128, 128), 128)

    barrier = pltpu.get_barrier_semaphore()

    def greet(to):
        pl.semaphore_signal(barrier, inc=1, device_id=to, device_id_type=MESH)

    memory = [
        pltpu.make_async_copy(src, dst, loc.at[2, n + 2]) for n, (src, dst) in enumerate(((keys_in, k), (values_in, v)))
    ]
    for copy in memory:
        copy.start()

    @pl.loop(0, 16)
    def _(i):
        @pl.when(jnp.logical_not(is_me(i)))
        def _():
            greet(workers(i)[1])
            greet(owners(i))

    for t in range(TILES):

        @pl.loop(0, PER_TILE - t)
        def _(k):
            greet(group(t, k, 1)[1])

    for d in (1, -1, 2, -2):
        greet(along(d))

    mine = []
    for h in range(2):
        for n, (src, dst) in enumerate(((q, qb), (g, gb))):
            mine.append(pltpu.make_async_copy(src.at[:, columns(pair, h)], dst.at[h, SELF], loc.at[n, h]))
            mine[-1].start()
    for copy in memory:
        copy.wait()
    for h in range(4):
        kvsrc[h] = jnp.concatenate(
            [k[:, h * DH : (h + 1) * DH].astype(F32), v[:, h * DH : (h + 1) * DH].astype(F32)], axis=0
        ).astype(BF16)

    pl.semaphore_wait(barrier, 51 - 2 * to_itself.astype(jnp.int32))

    for head in range(2):

        @pl.loop(0, 16)
        def _(i):
            j, to = workers(i)
            one = kvsrc.at[j * 2 + head]
            dst = kv.at[head, 0, yh * 8 + z]

            @pl.when(jnp.logical_not(is_me(i)))
            def _():
                remote(one, dst, kv1_send.at[head], kv1_recv.at[head], to).start()

            @pl.when(is_me(i))
            def _():
                copy = pltpu.make_async_copy(one, dst, loc.at[2, 0])
                copy.start()
                copy.wait()

    def share(h):
        for t in range(TILES):

            @pl.loop(0, PER_TILE - t)
            def _(k):
                i, to, theirs = group(t, k, 1)
                for n, (src, dst) in enumerate(((q, qb), (g, gb))):
                    remote(src.at[:, columns(theirs, h)], dst.at[h, i], in_send.at[n], in_recv.at[h, t, n], to).start()

    share(0)
    lower, upper = pl.ds(0, 8), pl.ds(8, 8)
    for h in range(2):
        memory_blocks(kv.at[h, 0], kv1_recv.at[h])
        if h == 1:
            bytes_of(kv.at[0, pl.ds(0, 3)], kv2_send.at[0])
        for piece, d in ((lower, 2), (upper, -2), (pl.ds(0, 16), 1), (pl.ds(0, 16), -1)):
            there = kv.at[h, (4 - d) % 4, piece]
            remote(kv.at[h, 0, piece], there, kv2_send.at[h], kv2_recv.at[h], along(d)).start()
        if h == 0:
            share(1)

    flows = ((pb, vt, attb, att), (dsb, kt, dqb, dq))

    def result(h, t, n):
        weights, other, buffer, _ = flows[n]
        made = jnp.dot(other[...], weights[t].reshape(512, TILE), preferred_element_type=F32)
        buffer[h, t * PER_TILE : (t + 1) * PER_TILE] = made.T.astype(BF16).reshape(PER_TILE, TOKENS, DH)

    def send(h, t, n):
        _, _, buffer, whole = flows[n]
        target = whole.at[:, columns(pair, h)]

        @pl.loop(0, PER_TILE - t)
        def _(k):
            i, to, _ = group(t, k, -1)
            remote(buffer.at[h, i], target, out_send.at[n], out_recv.at[n], to).start()

        if t == SELF // PER_TILE:
            pltpu.make_async_copy(buffer.at[h, SELF], target, loc.at[n, 2 + h]).start()

    for h in range(2):
        bytes_of(kv.at[h, pl.ds(1, 3)], kv2_recv.at[h])
        both = kv[h].reshape(64, 16, DH).astype(F32)
        keys = both[:, :8].reshape(512, DH)
        values = both[:, 8:].reshape(512, DH)
        kc[...] = keys.astype(BF16)
        vc[...] = values.astype(BF16)
        kt[...] = keys.T.astype(BF16)
        vt[...] = values.T.astype(BF16)
        for t in range(TILES):
            if t == SELF // PER_TILE:
                for copy in mine[2 * h : 2 * h + 2]:
                    copy.wait()
            for n, dst in enumerate((qb, gb)):
                bytes_of(dst.at[h, pl.ds(0, 7 if t == SELF // PER_TILE else 8)], in_recv.at[h, t, n])
            rows = pl.ds(t * PER_TILE, PER_TILE)
            qt = qb[h, rows].reshape(TILE, DH)
            gt = gb[h, rows].reshape(TILE, DH)
            s = lax.dot_general(kc[...], qt, NT, preferred_element_type=F32)
            dp = lax.dot_general(vc[...], gt, NT, preferred_element_type=F32)
            top = jnp.max(s, axis=0, keepdims=True)
            e = jnp.exp2((s - top) * (TEMPER * LOG2E))
            inverse = 1.0 / jnp.sum(e, axis=0, keepdims=True)
            delta = jnp.sum(e * dp, axis=0, keepdims=True) * inverse
            pb[t] = (e * inverse).astype(BF16).reshape(4, 128, TILE)
            dsb[t] = (e * (dp - delta) * (inverse * TEMPER)).astype(BF16).reshape(4, 128, TILE)
            if h == 0:
                for n in range(2):
                    result(h, t, n)
                    send(h, t, n)
        queries, grads = qb[h].reshape(16 * TOKENS, DH), gb[h].reshape(16 * TOKENS, DH)
        for d in (2, 1, 3, 0):
            dk, dv = (
                jnp.dot(weights[0, d], other[:TILE], preferred_element_type=F32)
                + jnp.dot(weights[1, d], other[TILE:], preferred_element_type=F32)
                for weights, other in ((dsb, queries), (pb, grads))
            )
            sums = jnp.concatenate([dk.reshape(16, 8, DH), dv.reshape(16, 8, DH)], axis=1)
            if d == 0:
                own[h] = sums
                continue
            part[h, d - 1] = sums.astype(BF16)
            for half in range(2):
                slots = pl.ds(half * 8, 8)
                if d == 2:
                    to, land = along(2 if half else -2), landh.at[h, half]
                else:
                    to, land = along(1 if d == 1 else -1), landf.at[h, d // 2, slots]
                remote(part.at[h, d - 1, slots], land, a_send.at[h], a_recv.at[h, half], to).start()

    def gather_sums(h, half):
        slots = pl.ds(half * 8, 8)
        bytes_of(part.at[h, :, slots], a_recv.at[h, half])
        total = own[h, slots] + landf[h, 0, slots].astype(F32) + landf[h, 1, slots].astype(F32)
        total += landh[h, half].astype(F32)
        red[h, slots] = total.astype(BF16)

        @pl.loop(half * 8, half * 8 + 8)
        def _(i):
            dst = landb.at[yh * 4 + zp, zb * 2 + h]

            @pl.when(jnp.logical_not(is_me(i)))
            def _():
                remote(red.at[h, i], dst, b_send.at[h], b_recv.at[h], owners(i)).start()

            @pl.when(is_me(i))
            def _():
                copy = pltpu.make_async_copy(red.at[h, i], dst, loc.at[2, 1])
                copy.start()
                copy.wait()

    gather_sums(0, 0)
    gather_sums(0, 1)
    for t in range(TILES):
        result(1, t, 0)
        send(1, t, 0)
    for t in range(TILES):
        result(1, t, 1)
    gather_sums(1, 0)
    gather_sums(1, 1)
    for t in range(TILES):
        send(1, t, 1)

    for n, (src, dst) in enumerate(((attb, att), (dqb, dq))):
        for h in range(2):
            pltpu.make_async_copy(src.at[h, SELF], dst.at[:, columns(pair, h)], loc.at[n, 2 + h]).wait()

    for h in range(2):
        for sem in (b_recv, b_send, kv1_send):
            memory_blocks(red.at[h], sem.at[h])

    bytes_of(kv.at[1, pl.ds(0, 3)], kv2_send.at[1])
    for n in range(2):
        bytes_of(attb.at[:, pl.ds(0, 15)], out_recv.at[n])
        bytes_of(attb.at[:, pl.ds(0, 15)], out_send.at[n])
        bytes_of(qb.at[:, pl.ds(0, 15)], in_send.at[n])
        bytes_of(part.at[n], a_send.at[n])


def finish(att_in, dq_in, landb, att, dq, kg, vg, sems):
    copies = [
        pltpu.make_async_copy(src.at[pl.ds(r * 16, 16)], dst.at[pl.ds(r * 16, 16)], sems.at[n, r])
        for r in range(4)
        for n, (src, dst) in enumerate(((att_in, att), (dq_in, dq)))
    ]
    for copy in copies:
        copy.start()
    final = landb[0].astype(F32)
    for n in range(1, 8):
        final += landb[n].astype(F32)
    for h in range(4):
        kg[:, h * DH : (h + 1) * DH] = final[h, :8].astype(BF16)
        vg[:, h * DH : (h + 1) * DH] = final[h, 8:].astype(BF16)
    for copy in copies:
        copy.wait()


def shards(queries, memory_keys, memory_values, output_grad):
    vmem, hbm = pl.BlockSpec(memory_space=pltpu.VMEM), pl.BlockSpec(memory_space=pl.ANY)
    tokens, memory = jax.ShapeDtypeStruct((64, 4096), BF16), jax.ShapeDtypeStruct((8, 512), BF16)
    dma = pltpu.SemaphoreType.DMA
    att, dq, landb = pl.pallas_call(
        kernel,
        name="attention",
        out_shape=(pltpu.VMEM((64, 4096), BF16), pltpu.VMEM((64, 4096), BF16), pltpu.VMEM((8, 4, 16, DH), BF16)),
        in_specs=[hbm] * 4,
        out_specs=(vmem, vmem, vmem),
        scratch_shapes=[
            pltpu.VMEM((8, 512), BF16),
            pltpu.VMEM((8, 512), BF16),
            pltpu.VMEM((2, 16, TOKENS, DH), BF16),
            pltpu.VMEM((2, 16, TOKENS, DH), BF16),
            pltpu.VMEM((4, 16, DH), BF16),
            pltpu.VMEM((2, 4, 16, 16, DH), BF16),
            pltpu.VMEM((2, 16, TOKENS, DH), BF16),
            pltpu.VMEM((2, 16, TOKENS, DH), BF16),
            pltpu.VMEM((512, DH), BF16),
            pltpu.VMEM((512, DH), BF16),
            pltpu.VMEM((DH, 512), BF16),
            pltpu.VMEM((DH, 512), BF16),
            pltpu.VMEM((TILES, 4, 128, TILE), BF16),
            pltpu.VMEM((TILES, 4, 128, TILE), BF16),
            pltpu.VMEM((2, 3, 16, 16, DH), BF16),
            pltpu.VMEM((2, 16, 16, DH), F32),
            pltpu.VMEM((2, 2, 16, 16, DH), BF16),
            pltpu.VMEM((2, 2, 8, 16, DH), BF16),
            pltpu.VMEM((2, 16, 16, DH), BF16),
            dma((2,)),
            dma((2, TILES, 2)),
            dma((3, 4)),
            dma((2,)),
            dma((2,)),
            dma((2,)),
            dma((2,)),
            dma((2,)),
            dma((2,)),
            dma((2,)),
            dma((2, 2)),
            dma((2,)),
            dma((2,)),
        ],
        compiler_params=pltpu.CompilerParams(
            collective_id=0, has_side_effects=True, vmem_limit_bytes=60 * 2**20
        ),
    )(queries, memory_keys, memory_values, output_grad)
    return pl.pallas_call(
        finish,
        name="finish",
        out_shape=(tokens, tokens, memory, memory),
        in_specs=[vmem, vmem, vmem],
        out_specs=(hbm, hbm, vmem, vmem),
        scratch_shapes=[dma((2, 4))],
    )(*(pltpu.with_memory_space_constraint(t, pltpu.VMEM) for t in (att, dq, landb)))


def solution(mesh):
    return jax.shard_map(
        shards,
        mesh=mesh,
        in_specs=(P(("seq", "mp"), None), P("seq", "mp"), P("seq", "mp"), P(("seq", "mp"), None)),
        out_specs=(P(("seq", "mp"), None), P(("seq", "mp"), None), P("seq", "mp"), P("seq", "mp")),
        check_vma=False,
    )
```

```python
import math

import jax
import jax.numpy as jnp
from jax import lax
from jax.experimental import pallas as pl
from jax.experimental.pallas import tpu as pltpu
from jax.sharding import PartitionSpec as P

MESH = pl.DeviceIdType.MESH
DH = 128
TEMPER = 1.0 / math.sqrt(DH)
LOG2E = 1.0 / math.log(2.0)
NT = (((1,), (1,)), ((), ()))
BF16, F32 = jnp.bfloat16, jnp.float32
TILES, PER_TILE, TOKENS = 2, 8, 64
SELF = 12
TILE = PER_TILE * TOKENS


def place():
    seq, mp = lax.axis_index("seq"), lax.axis_index("mp")
    return seq % 4, (seq // 32) * 4 + mp // 2, (seq // 4) % 8, mp % 2


def device(x, y, z, core):
    return (y // 4) * 32 + z * 4 + x, (y % 4) * 2 + core


def kernel(
    q, keys_in, values_in, g, att, dq, landb,
    k, v, qb, gb, kvsrc, kv, attb, dqb, kc, vc, kt, vt, pb, dsb, part, own, landf, landh, red,
    in_send, in_recv, loc, kv1_send, kv1_recv, kv2_send, kv2_recv, out_send, out_recv,
    a_send, a_recv, b_send, b_recv,
):
    x, y, z, core = place()
    yh, a = y // 4, y % 4
    zp, zb = z // 2, z % 2
    block = (x + 4 - zp) % 4
    pair = 4 * block + 2 * core + zb
    place_in_block = (x + z) % 4
    to_itself = (block == a) & (place_in_block == a)

    def group(t, k, sign):
        odd, m = k % 2, k // 2 + (k % 2) * t
        dx = 1 + 2 * odd if t == 0 else 2 - 2 * odd
        dz, dc = m // 2, m % 2
        xx, bb, cc = (x + sign * dx + 4) % 4, (zb + dz) % 2, (core + dc) % 2
        return t * PER_TILE + odd * 4 + m, device(xx, y, 2 * zp + bb, cc), 4 * ((xx + 4 - zp) % 4) + 2 * cc + bb

    def workers(i):
        h, zz = i // 8, i % 8
        return zz % 2, device((a + zz // 2) % 4, 4 * h + place_in_block, zz, core)

    def owners(i):
        h, zz = i // 8, i % 8
        return device((a + 8 - zz) % 4, 4 * h + block, zz, core)

    def along(d):
        return device(x, (y + d + 8) % 8, z, core)

    def remote(src, dst, send, recv, to):
        return pltpu.make_async_remote_copy(
            src_ref=src, dst_ref=dst, send_sem=send, recv_sem=recv, device_id=to, device_id_type=MESH
        )

    def bytes_of(ref, sem):
        pltpu.make_async_copy(ref, ref, sem).wait()

    def memory_blocks(ref, sem):
        @pl.when(to_itself)
        def _():
            bytes_of(ref.at[pl.ds(0, 15)], sem)

        @pl.when(jnp.logical_not(to_itself))
        def _():
            bytes_of(ref, sem)

    def far_first(n):
        step = (n + 1) // 2
        return (z + 12 + step * (2 * (n % 2) - 1)) % 8

    def is_me(i):
        return to_itself & (i // 8 == yh) & (i % 8 == z)

    def columns(head_pair, head):
        return pl.ds(pl.multiple_of(head_pair * 256 + head * 128, 128), 128)

    barrier = pltpu.get_barrier_semaphore()

    def greet(to):
        pl.semaphore_signal(barrier, inc=1, device_id=to, device_id_type=MESH)

    memory = [
        pltpu.make_async_copy(src, dst, loc.at[2, n + 2]) for n, (src, dst) in enumerate(((keys_in, k), (values_in, v)))
    ]
    for copy in memory:
        copy.start()

    @pl.loop(0, 16)
    def _(i):
        @pl.when(jnp.logical_not(is_me(i)))
        def _():
            greet(workers(i)[1])
            greet(owners(i))

    for t in range(TILES):

        @pl.loop(0, PER_TILE - t)
        def _(k):
            greet(group(t, k, 1)[1])

    for d in (1, -1, 2, -2):
        greet(along(d))

    mine = []
    for h in range(2):
        for n, (src, dst) in enumerate(((q, qb), (g, gb))):
            mine.append(pltpu.make_async_copy(src.at[:, columns(pair, h)], dst.at[h, SELF], loc.at[n, h]))
            mine[-1].start()
    for copy in memory:
        copy.wait()
    for h in range(4):
        kvsrc[h] = jnp.concatenate(
            [k[:, h * DH : (h + 1) * DH].astype(F32), v[:, h * DH : (h + 1) * DH].astype(F32)], axis=0
        ).astype(BF16)

    pl.semaphore_wait(barrier, 51 - 2 * to_itself.astype(jnp.int32))

    for head in range(2):

        @pl.loop(0, 16)
        def _(n):
            i = ((yh + 1 + n) % 2) * 8 + far_first(n // 2)
            j, to = workers(i)
            one = kvsrc.at[j * 2 + head]
            dst = kv.at[head, 0, yh * 8 + z]

            @pl.when(jnp.logical_not(is_me(i)))
            def _():
                remote(one, dst, kv1_send.at[head], kv1_recv.at[head], to).start()

            @pl.when(is_me(i))
            def _():
                copy = pltpu.make_async_copy(one, dst, loc.at[2, 0])
                copy.start()
                copy.wait()

    def share(h):
        for t in range(TILES):

            @pl.loop(0, PER_TILE - t)
            def _(k):
                i, to, theirs = group(t, k, 1)
                for n, (src, dst) in enumerate(((q, qb), (g, gb))):
                    remote(src.at[:, columns(theirs, h)], dst.at[h, i], in_send.at[n], in_recv.at[h, t, n], to).start()

    share(0)
    lower, upper = pl.ds(0, 8), pl.ds(8, 8)
    for h in range(2):
        memory_blocks(kv.at[h, 0], kv1_recv.at[h])
        if h == 1:
            bytes_of(kv.at[0, pl.ds(0, 3)], kv2_send.at[0])
        for piece, d in ((lower, 2), (upper, -2), (pl.ds(0, 16), 1), (pl.ds(0, 16), -1)):
            there = kv.at[h, (4 - d) % 4, piece]
            remote(kv.at[h, 0, piece], there, kv2_send.at[h], kv2_recv.at[h], along(d)).start()
        if h == 0:
            share(1)

    flows = ((pb, vt, attb, att), (dsb, kt, dqb, dq))

    def result(h, t, n):
        weights, other, buffer, _ = flows[n]
        made = jnp.dot(other[...], weights[t].reshape(512, TILE), preferred_element_type=F32)
        buffer[h, t * PER_TILE : (t + 1) * PER_TILE] = made.T.astype(BF16).reshape(PER_TILE, TOKENS, DH)

    def send(h, t, n):
        _, _, buffer, whole = flows[n]
        target = whole.at[:, columns(pair, h)]

        @pl.loop(0, PER_TILE - t)
        def _(k):
            i, to, _ = group(t, k, -1)
            remote(buffer.at[h, i], target, out_send.at[n], out_recv.at[n], to).start()

        if t == SELF // PER_TILE:
            pltpu.make_async_copy(buffer.at[h, SELF], target, loc.at[n, 2 + h]).start()

    for h in range(2):
        bytes_of(kv.at[h, pl.ds(1, 3)], kv2_recv.at[h])
        both = kv[h].reshape(64, 16, DH).astype(F32)
        keys = both[:, :8].reshape(512, DH)
        values = both[:, 8:].reshape(512, DH)
        kc[...] = keys.astype(BF16)
        vc[...] = values.astype(BF16)
        kt[...] = keys.T.astype(BF16)
        vt[...] = values.T.astype(BF16)
        for t in range(TILES):
            if t == SELF // PER_TILE:
                for copy in mine[2 * h : 2 * h + 2]:
                    copy.wait()
            for n, dst in enumerate((qb, gb)):
                bytes_of(dst.at[h, pl.ds(0, 7 if t == SELF // PER_TILE else 8)], in_recv.at[h, t, n])
            rows = pl.ds(t * PER_TILE, PER_TILE)
            qt = qb[h, rows].reshape(TILE, DH)
            gt = gb[h, rows].reshape(TILE, DH)
            s = lax.dot_general(kc[...], qt, NT, preferred_element_type=F32)
            dp = lax.dot_general(vc[...], gt, NT, preferred_element_type=F32)
            top = jnp.max(s, axis=0, keepdims=True)
            e = jnp.exp2((s - top) * (TEMPER * LOG2E))
            inverse = 1.0 / jnp.sum(e, axis=0, keepdims=True)
            delta = jnp.sum(e * dp, axis=0, keepdims=True) * inverse
            pb[t] = (e * inverse).astype(BF16).reshape(4, 128, TILE)
            dsb[t] = (e * (dp - delta) * (inverse * TEMPER)).astype(BF16).reshape(4, 128, TILE)
            if h == 0:
                for n in range(2):
                    result(h, t, n)
                    send(h, t, n)
        queries, grads = qb[h].reshape(16 * TOKENS, DH), gb[h].reshape(16 * TOKENS, DH)
        for d in (2, 1, 3, 0):
            dk, dv = (
                jnp.dot(weights[0, d], other[:TILE], preferred_element_type=F32)
                + jnp.dot(weights[1, d], other[TILE:], preferred_element_type=F32)
                for weights, other in ((dsb, queries), (pb, grads))
            )
            sums = jnp.concatenate([dk.reshape(16, 8, DH), dv.reshape(16, 8, DH)], axis=1)
            if d == 0:
                own[h] = sums
                continue
            part[h, d - 1] = sums.astype(BF16)
            for half in range(2):
                slots = pl.ds(half * 8, 8)
                if d == 2:
                    to, land = along(2 if half else -2), landh.at[h, half]
                else:
                    to, land = along(1 if d == 1 else -1), landf.at[h, d // 2, slots]
                remote(part.at[h, d - 1, slots], land, a_send.at[h], a_recv.at[h, half], to).start()

    def gather_sums(h, half):
        slots = pl.ds(half * 8, 8)
        bytes_of(part.at[h, :, slots], a_recv.at[h, half])
        total = own[h, slots] + landf[h, 0, slots].astype(F32) + landf[h, 1, slots].astype(F32)
        total += landh[h, half].astype(F32)
        red[h, slots] = total.astype(BF16)

        @pl.loop(0, 8)
        def _(n):
            i = half * 8 + far_first(n)
            dst = landb.at[yh * 4 + zp, zb * 2 + h]

            @pl.when(jnp.logical_not(is_me(i)))
            def _():
                remote(red.at[h, i], dst, b_send.at[h], b_recv.at[h], owners(i)).start()

            @pl.when(is_me(i))
            def _():
                copy = pltpu.make_async_copy(red.at[h, i], dst, loc.at[2, 1])
                copy.start()
                copy.wait()

    gather_sums(0, 0)
    gather_sums(0, 1)
    for t in range(TILES):
        result(1, t, 0)
        send(1, t, 0)
    for t in range(TILES):
        result(1, t, 1)
    gather_sums(1, 0)
    gather_sums(1, 1)
    for t in range(TILES):
        send(1, t, 1)

    for n, (src, dst) in enumerate(((attb, att), (dqb, dq))):
        for h in range(2):
            pltpu.make_async_copy(src.at[h, SELF], dst.at[:, columns(pair, h)], loc.at[n, 2 + h]).wait()

    for h in range(2):
        for sem in (b_recv, b_send, kv1_send):
            memory_blocks(red.at[h], sem.at[h])

    bytes_of(kv.at[1, pl.ds(0, 3)], kv2_send.at[1])
    for n in range(2):
        bytes_of(attb.at[:, pl.ds(0, 15)], out_recv.at[n])
        bytes_of(attb.at[:, pl.ds(0, 15)], out_send.at[n])
        bytes_of(qb.at[:, pl.ds(0, 15)], in_send.at[n])
        bytes_of(part.at[n], a_send.at[n])


def finish(att_in, dq_in, landb, att, dq, kg, vg, kg_made, vg_made, sems):
    copies = [
        pltpu.make_async_copy(src, dst, sems.at[n])
        for n, (src, dst) in enumerate(((att_in, att), (dq_in, dq), (kg_made, kg), (vg_made, vg)))
    ]
    for copy in copies[:2]:
        copy.start()
    final = landb[0].astype(F32)
    for n in range(1, 8):
        final += landb[n].astype(F32)
    for h in range(4):
        kg_made[:, h * DH : (h + 1) * DH] = final[h, :8].astype(BF16)
        vg_made[:, h * DH : (h + 1) * DH] = final[h, 8:].astype(BF16)
    for copy in copies[2:]:
        copy.start()
    for copy in copies:
        copy.wait()


def shards(queries, memory_keys, memory_values, output_grad):
    vmem, hbm = pl.BlockSpec(memory_space=pltpu.VMEM), pl.BlockSpec(memory_space=pl.ANY)
    tokens, memory = jax.ShapeDtypeStruct((64, 4096), BF16), jax.ShapeDtypeStruct((8, 512), BF16)
    dma = pltpu.SemaphoreType.DMA
    att, dq, landb = pl.pallas_call(
        kernel,
        name="attention",
        out_shape=(pltpu.VMEM((64, 4096), BF16), pltpu.VMEM((64, 4096), BF16), pltpu.VMEM((8, 4, 16, DH), BF16)),
        in_specs=[hbm] * 4,
        out_specs=(vmem, vmem, vmem),
        scratch_shapes=[
            pltpu.VMEM((8, 512), BF16),
            pltpu.VMEM((8, 512), BF16),
            pltpu.VMEM((2, 16, TOKENS, DH), BF16),
            pltpu.VMEM((2, 16, TOKENS, DH), BF16),
            pltpu.VMEM((4, 16, DH), BF16),
            pltpu.VMEM((2, 4, 16, 16, DH), BF16),
            pltpu.VMEM((2, 16, TOKENS, DH), BF16),
            pltpu.VMEM((2, 16, TOKENS, DH), BF16),
            pltpu.VMEM((512, DH), BF16),
            pltpu.VMEM((512, DH), BF16),
            pltpu.VMEM((DH, 512), BF16),
            pltpu.VMEM((DH, 512), BF16),
            pltpu.VMEM((TILES, 4, 128, TILE), BF16),
            pltpu.VMEM((TILES, 4, 128, TILE), BF16),
            pltpu.VMEM((2, 3, 16, 16, DH), BF16),
            pltpu.VMEM((2, 16, 16, DH), F32),
            pltpu.VMEM((2, 2, 16, 16, DH), BF16),
            pltpu.VMEM((2, 2, 8, 16, DH), BF16),
            pltpu.VMEM((2, 16, 16, DH), BF16),
            dma((2,)),
            dma((2, TILES, 2)),
            dma((3, 4)),
            dma((2,)),
            dma((2,)),
            dma((2,)),
            dma((2,)),
            dma((2,)),
            dma((2,)),
            dma((2,)),
            dma((2, 2)),
            dma((2,)),
            dma((2,)),
        ],
        compiler_params=pltpu.CompilerParams(
            collective_id=0, has_side_effects=True, vmem_limit_bytes=60 * 2**20
        ),
    )(queries, memory_keys, memory_values, output_grad)
    return pl.pallas_call(
        finish,
        name="finish",
        out_shape=(tokens, tokens, memory, memory),
        in_specs=[vmem, vmem, vmem],
        out_specs=(hbm, hbm, hbm, hbm),
        scratch_shapes=[pltpu.VMEM((8, 512), BF16), pltpu.VMEM((8, 512), BF16), dma((4,))],
    )(*(pltpu.with_memory_space_constraint(t, pltpu.VMEM) for t in (att, dq, landb)))


def solution(mesh):
    return jax.shard_map(
        shards,
        mesh=mesh,
        in_specs=(P(("seq", "mp"), None), P("seq", "mp"), P("seq", "mp"), P(("seq", "mp"), None)),
        out_specs=(P(("seq", "mp"), None), P(("seq", "mp"), None), P("seq", "mp"), P("seq", "mp")),
        check_vma=False,
    )
```

```python
import math

import jax
import jax.numpy as jnp
from jax import lax
from jax.experimental import pallas as pl
from jax.experimental.pallas import tpu as pltpu
from jax.sharding import PartitionSpec as P

MESH = pl.DeviceIdType.MESH
DH = 128
TEMPER = 1.0 / math.sqrt(DH)
LOG2E = 1.0 / math.log(2.0)
NT = (((1,), (1,)), ((), ()))
BF16, F32 = jnp.bfloat16, jnp.float32
TILES, PER_TILE, TOKENS = 2, 8, 64
SELF = 12
TILE = PER_TILE * TOKENS


def place():
    seq, mp = lax.axis_index("seq"), lax.axis_index("mp")
    return seq % 4, (seq // 32) * 4 + mp // 2, (seq // 4) % 8, mp % 2


def device(x, y, z, core):
    return (y // 4) * 32 + z * 4 + x, (y % 4) * 2 + core


def kernel(
    q, keys_in, values_in, g, att, dq, landb,
    k, v, qb, gb, kvsrc, kv, attb, dqb, kc, vc, kt, vt, pb, dsb, part, own, landf, landh, red,
    in_send, in_recv, loc, kv1_send, kv1_recv, kv2_send, kv2_recv, out_send, out_recv,
    a_send, a_recv, b_send, b_recv,
):
    x, y, z, core = place()
    yh, a = y // 4, y % 4
    zp, zb = z // 2, z % 2
    block = (x + 4 - zp) % 4
    pair = 4 * block + 2 * core + zb
    place_in_block = (x + z) % 4
    to_itself = (block == a) & (place_in_block == a)

    def group(t, k, sign):
        odd, m = k % 2, k // 2 + (k % 2) * t
        dx = 1 + 2 * odd if t == 0 else 2 - 2 * odd
        dz, dc = m // 2, m % 2
        xx, bb, cc = (x + sign * dx + 4) % 4, (zb + dz) % 2, (core + dc) % 2
        return t * PER_TILE + odd * 4 + m, device(xx, y, 2 * zp + bb, cc), 4 * ((xx + 4 - zp) % 4) + 2 * cc + bb

    def workers(i):
        h, zz = i // 8, i % 8
        return zz % 2, device((a + zz // 2) % 4, 4 * h + place_in_block, zz, core)

    def owners(i):
        h, zz = i // 8, i % 8
        return device((a + 8 - zz) % 4, 4 * h + block, zz, core)

    def along(d):
        return device(x, (y + d + 8) % 8, z, core)

    def remote(src, dst, send, recv, to):
        return pltpu.make_async_remote_copy(
            src_ref=src, dst_ref=dst, send_sem=send, recv_sem=recv, device_id=to, device_id_type=MESH
        )

    def bytes_of(ref, sem):
        pltpu.make_async_copy(ref, ref, sem).wait()

    def memory_blocks(ref, sem):
        @pl.when(to_itself)
        def _():
            bytes_of(ref.at[pl.ds(0, 15)], sem)

        @pl.when(jnp.logical_not(to_itself))
        def _():
            bytes_of(ref, sem)

    def far_first(n):
        step = (n + 1) // 2
        return (z + 12 + step * (2 * (n % 2) - 1)) % 8

    def is_me(i):
        return to_itself & (i // 8 == yh) & (i % 8 == z)

    def columns(head_pair, head):
        return pl.ds(pl.multiple_of(head_pair * 256 + head * 128, 128), 128)

    barrier = pltpu.get_barrier_semaphore()

    def greet(to):
        pl.semaphore_signal(barrier, inc=1, device_id=to, device_id_type=MESH)

    memory = [
        pltpu.make_async_copy(src, dst, loc.at[2, n + 2]) for n, (src, dst) in enumerate(((keys_in, k), (values_in, v)))
    ]
    for copy in memory:
        copy.start()

    @pl.loop(0, 16)
    def _(n):
        i = ((yh + 1 + n) % 2) * 8 + far_first(n // 2)

        @pl.when(jnp.logical_not(is_me(i)))
        def _():
            greet(workers(i)[1])
            greet(owners(i))

    for t in range(TILES):

        @pl.loop(0, PER_TILE - t)
        def _(k):
            greet(group(t, k, 1)[1])

    for d in (1, -1, 2, -2):
        greet(along(d))

    mine = []
    for h in range(2):
        for n, (src, dst) in enumerate(((q, qb), (g, gb))):
            mine.append(pltpu.make_async_copy(src.at[:, columns(pair, h)], dst.at[h, SELF], loc.at[n, h]))
            mine[-1].start()
    for copy in memory:
        copy.wait()
    for h in range(4):
        kvsrc[h] = jnp.concatenate(
            [k[:, h * DH : (h + 1) * DH].astype(F32), v[:, h * DH : (h + 1) * DH].astype(F32)], axis=0
        ).astype(BF16)

    pl.semaphore_wait(barrier, 51 - 2 * to_itself.astype(jnp.int32))

    for head in range(2):

        @pl.loop(0, 16)
        def _(n):
            i = ((yh + 1 + n) % 2) * 8 + far_first(n // 2)
            j, to = workers(i)
            one = kvsrc.at[j * 2 + head]
            dst = kv.at[head, 0, yh * 8 + z]

            @pl.when(jnp.logical_not(is_me(i)))
            def _():
                remote(one, dst, kv1_send.at[head], kv1_recv.at[head], to).start()

            @pl.when(is_me(i))
            def _():
                copy = pltpu.make_async_copy(one, dst, loc.at[2, 0])
                copy.start()
                copy.wait()

    def share(h):
        for t in range(TILES):

            @pl.loop(0, PER_TILE - t)
            def _(k):
                i, to, theirs = group(t, k, 1)
                for n, (src, dst) in enumerate(((q, qb), (g, gb))):
                    remote(src.at[:, columns(theirs, h)], dst.at[h, i], in_send.at[n], in_recv.at[h, t, n], to).start()

    share(0)
    lower, upper = pl.ds(0, 8), pl.ds(8, 8)
    for h in range(2):
        memory_blocks(kv.at[h, 0], kv1_recv.at[h])
        if h == 1:
            bytes_of(kv.at[0, pl.ds(0, 3)], kv2_send.at[0])
        for piece, d in ((lower, 2), (upper, -2), (pl.ds(0, 16), 1), (pl.ds(0, 16), -1)):
            there = kv.at[h, (4 - d) % 4, piece]
            remote(kv.at[h, 0, piece], there, kv2_send.at[h], kv2_recv.at[h], along(d)).start()
        if h == 0:
            share(1)

    flows = ((pb, vt, attb, att), (dsb, kt, dqb, dq))

    def result(h, t, n):
        weights, other, buffer, _ = flows[n]
        made = jnp.dot(other[...], weights[t].reshape(512, TILE), preferred_element_type=F32)
        buffer[h, t * PER_TILE : (t + 1) * PER_TILE] = made.T.astype(BF16).reshape(PER_TILE, TOKENS, DH)

    def send(h, t, n):
        _, _, buffer, whole = flows[n]
        target = whole.at[:, columns(pair, h)]

        @pl.loop(0, PER_TILE - t)
        def _(k):
            i, to, _ = group(t, k, -1)
            remote(buffer.at[h, i], target, out_send.at[n], out_recv.at[n], to).start()

        if t == SELF // PER_TILE:
            pltpu.make_async_copy(buffer.at[h, SELF], target, loc.at[n, 2 + h]).start()

    for h in range(2):
        bytes_of(kv.at[h, pl.ds(1, 3)], kv2_recv.at[h])
        both = kv[h].reshape(64, 16, DH).astype(F32)
        keys = both[:, :8].reshape(512, DH)
        values = both[:, 8:].reshape(512, DH)
        kc[...] = keys.astype(BF16)
        vc[...] = values.astype(BF16)
        kt[...] = keys.T.astype(BF16)
        vt[...] = values.T.astype(BF16)
        for t in range(TILES):
            if t == SELF // PER_TILE:
                for copy in mine[2 * h : 2 * h + 2]:
                    copy.wait()
            for n, dst in enumerate((qb, gb)):
                bytes_of(dst.at[h, pl.ds(0, 7 if t == SELF // PER_TILE else 8)], in_recv.at[h, t, n])
            rows = pl.ds(t * PER_TILE, PER_TILE)
            qt = qb[h, rows].reshape(TILE, DH)
            gt = gb[h, rows].reshape(TILE, DH)
            s = lax.dot_general(kc[...], qt, NT, preferred_element_type=F32)
            dp = lax.dot_general(vc[...], gt, NT, preferred_element_type=F32)
            top = jnp.max(s, axis=0, keepdims=True)
            e = jnp.exp2((s - top) * (TEMPER * LOG2E))
            inverse = 1.0 / jnp.sum(e, axis=0, keepdims=True)
            delta = jnp.sum(e * dp, axis=0, keepdims=True) * inverse
            pb[t] = (e * inverse).astype(BF16).reshape(4, 128, TILE)
            dsb[t] = (e * (dp - delta) * (inverse * TEMPER)).astype(BF16).reshape(4, 128, TILE)
            if h == 0:
                for n in range(2):
                    result(h, t, n)
                    send(h, t, n)
        queries, grads = qb[h].reshape(16 * TOKENS, DH), gb[h].reshape(16 * TOKENS, DH)
        for d in (2, 1, 3, 0):
            dk, dv = (
                jnp.dot(weights[0, d], other[:TILE], preferred_element_type=F32)
                + jnp.dot(weights[1, d], other[TILE:], preferred_element_type=F32)
                for weights, other in ((dsb, queries), (pb, grads))
            )
            sums = jnp.concatenate([dk.reshape(16, 8, DH), dv.reshape(16, 8, DH)], axis=1)
            if d == 0:
                own[h] = sums
                continue
            part[h, d - 1] = sums.astype(BF16)
            for half in range(2):
                slots = pl.ds(half * 8, 8)
                if d == 2:
                    to, land = along(2 if half else -2), landh.at[h, half]
                else:
                    to, land = along(1 if d == 1 else -1), landf.at[h, d // 2, slots]
                remote(part.at[h, d - 1, slots], land, a_send.at[h], a_recv.at[h, half], to).start()

    def gather_sums(h, half):
        slots = pl.ds(half * 8, 8)
        bytes_of(part.at[h, :, slots], a_recv.at[h, half])
        total = own[h, slots] + landf[h, 0, slots].astype(F32) + landf[h, 1, slots].astype(F32)
        total += landh[h, half].astype(F32)
        red[h, slots] = total.astype(BF16)

        @pl.loop(0, 8)
        def _(n):
            i = half * 8 + far_first(n)
            dst = landb.at[yh * 4 + zp, zb * 2 + h]

            @pl.when(jnp.logical_not(is_me(i)))
            def _():
                remote(red.at[h, i], dst, b_send.at[h], b_recv.at[h], owners(i)).start()

            @pl.when(is_me(i))
            def _():
                copy = pltpu.make_async_copy(red.at[h, i], dst, loc.at[2, 1])
                copy.start()
                copy.wait()

    gather_sums(0, 0)
    gather_sums(0, 1)
    for t in range(TILES):
        result(1, t, 0)
        send(1, t, 0)
    for t in range(TILES):
        result(1, t, 1)
    gather_sums(1, 0)
    gather_sums(1, 1)
    for t in range(TILES):
        send(1, t, 1)

    for n, (src, dst) in enumerate(((attb, att), (dqb, dq))):
        for h in range(2):
            pltpu.make_async_copy(src.at[h, SELF], dst.at[:, columns(pair, h)], loc.at[n, 2 + h]).wait()

    for h in range(2):
        for sem in (b_recv, b_send, kv1_send):
            memory_blocks(red.at[h], sem.at[h])

    bytes_of(kv.at[1, pl.ds(0, 3)], kv2_send.at[1])
    for n in range(2):
        bytes_of(attb.at[:, pl.ds(0, 15)], out_recv.at[n])
        bytes_of(attb.at[:, pl.ds(0, 15)], out_send.at[n])
        bytes_of(qb.at[:, pl.ds(0, 15)], in_send.at[n])
        bytes_of(part.at[n], a_send.at[n])


def finish(att_in, dq_in, landb, att, dq, kg, vg, kg_made, vg_made, sems):
    copies = [
        pltpu.make_async_copy(src, dst, sems.at[n])
        for n, (src, dst) in enumerate(((att_in, att), (dq_in, dq), (kg_made, kg), (vg_made, vg)))
    ]
    for copy in copies[:2]:
        copy.start()
    final = landb[0].astype(F32)
    for n in range(1, 8):
        final += landb[n].astype(F32)
    for h in range(4):
        kg_made[:, h * DH : (h + 1) * DH] = final[h, :8].astype(BF16)
        vg_made[:, h * DH : (h + 1) * DH] = final[h, 8:].astype(BF16)
    for copy in copies[2:]:
        copy.start()
    for copy in copies:
        copy.wait()


def shards(queries, memory_keys, memory_values, output_grad):
    vmem, hbm = pl.BlockSpec(memory_space=pltpu.VMEM), pl.BlockSpec(memory_space=pl.ANY)
    tokens, memory = jax.ShapeDtypeStruct((64, 4096), BF16), jax.ShapeDtypeStruct((8, 512), BF16)
    dma = pltpu.SemaphoreType.DMA
    att, dq, landb = pl.pallas_call(
        kernel,
        name="attention",
        out_shape=(pltpu.VMEM((64, 4096), BF16), pltpu.VMEM((64, 4096), BF16), pltpu.VMEM((8, 4, 16, DH), BF16)),
        in_specs=[hbm] * 4,
        out_specs=(vmem, vmem, vmem),
        scratch_shapes=[
            pltpu.VMEM((8, 512), BF16),
            pltpu.VMEM((8, 512), BF16),
            pltpu.VMEM((2, 16, TOKENS, DH), BF16),
            pltpu.VMEM((2, 16, TOKENS, DH), BF16),
            pltpu.VMEM((4, 16, DH), BF16),
            pltpu.VMEM((2, 4, 16, 16, DH), BF16),
            pltpu.VMEM((2, 16, TOKENS, DH), BF16),
            pltpu.VMEM((2, 16, TOKENS, DH), BF16),
            pltpu.VMEM((512, DH), BF16),
            pltpu.VMEM((512, DH), BF16),
            pltpu.VMEM((DH, 512), BF16),
            pltpu.VMEM((DH, 512), BF16),
            pltpu.VMEM((TILES, 4, 128, TILE), BF16),
            pltpu.VMEM((TILES, 4, 128, TILE), BF16),
            pltpu.VMEM((2, 3, 16, 16, DH), BF16),
            pltpu.VMEM((2, 16, 16, DH), F32),
            pltpu.VMEM((2, 2, 16, 16, DH), BF16),
            pltpu.VMEM((2, 2, 8, 16, DH), BF16),
            pltpu.VMEM((2, 16, 16, DH), BF16),
            dma((2,)),
            dma((2, TILES, 2)),
            dma((3, 4)),
            dma((2,)),
            dma((2,)),
            dma((2,)),
            dma((2,)),
            dma((2,)),
            dma((2,)),
            dma((2,)),
            dma((2, 2)),
            dma((2,)),
            dma((2,)),
        ],
        compiler_params=pltpu.CompilerParams(
            collective_id=0, has_side_effects=True, vmem_limit_bytes=60 * 2**20
        ),
    )(queries, memory_keys, memory_values, output_grad)
    return pl.pallas_call(
        finish,
        name="finish",
        out_shape=(tokens, tokens, memory, memory),
        in_specs=[vmem, vmem, vmem],
        out_specs=(hbm, hbm, hbm, hbm),
        scratch_shapes=[pltpu.VMEM((8, 512), BF16), pltpu.VMEM((8, 512), BF16), dma((4,))],
    )(*(pltpu.with_memory_space_constraint(t, pltpu.VMEM) for t in (att, dq, landb)))


def solution(mesh):
    return jax.shard_map(
        shards,
        mesh=mesh,
        in_specs=(P(("seq", "mp"), None), P("seq", "mp"), P("seq", "mp"), P(("seq", "mp"), None)),
        out_specs=(P(("seq", "mp"), None), P(("seq", "mp"), None), P("seq", "mp"), P("seq", "mp")),
        check_vma=False,
    )
```
